32 devices in a mesh: groups: 2 (over y), tp: 4 (over z), dp: 4 (over x, core).
Axes of the slice: x: 2, y: 2, z: 4, core: 2. Of those that a mesh axis runs over, the one named last changes fastest.
Arguments:
- queries: bfloat16 [8, 128, 1024], P(('groups', 'dp'), None, 'tp'), parts along dimension 0, may hold values from -90 to 90
- cache: bfloat16 [8, 4, 2, 3584, 128], P(('groups', 'dp'), 'tp'), parts along dimension 0, may hold values from -4.5 to 4.5
- new_kv: bfloat16 [8, 4, 2, 128, 128], P(('groups', 'dp'), 'tp'), parts along dimension 0, may hold values from -4.5 to 4.5
- out_weight: bfloat16 [1024, 4096], P('tp'), may hold values from -0.25 to 0.25
- prefix: int32 [8], P(('groups', 'dp')), parts along dimension 0, may hold values from 896 to 3584, as said below
Outputs:
- mixed: bfloat16 [8, 128, 4096], P(('groups', 'dp')), parts along dimension 0
The draws below stay inside these ranges and needn't reach their ends.
There are 2 independent parts, one for each index of `groups`. The reference program is written for one: setup_inputs(seed, part) draws one part's arguments, and reference() takes and returns one part's arrays. A program takes and returns all parts, laid end to end along the dimension named above; an argument that names none is the same for every part. Nothing has to cross between parts.
Inputs may be any that keep to these rules, and one draw needn't show every extreme that they name: `prefix`: the largest entry is 3584 in every draw.
All inputs are finite; a program needn't handle non-finite values. Where the reference program divides by a largest or mean magnitude, that divisor is 1e-20 or more.
Results may differ from the reference program's by a relative error of at most 0.014.
Values may be sent and summed in bfloat16 or wider, within the bound.
A program may use at most 64 MiB of HBM per device.

```python
import jax
import jax.numpy as jnp
from jax import lax

DW = 4096
HD = 128
HQ_DEV = 2
BLOCK = 128
CH = 128
PMAX = 3584
HQ = 8
REQS = 4
N_TP = 4


def shared_normal(key):
    return jnp.clip(jax.random.normal(key, (REQS, N_TP, 2, PMAX, HD), jnp.float32), -4.5, 4.5)


def draw_cache(key, part):
    past_kv = shared_normal(key)
    return past_kv.astype(jnp.bfloat16)


def draw_queries(key, part):
    key = jax.random.fold_in(key, 5)
    drawn = jnp.clip(jax.random.normal(key, (REQS, CH, N_TP, HQ_DEV, HD), jnp.float32), -4.5, 4.5)
    return drawn.reshape(REQS, CH, HQ * HD).astype(jnp.bfloat16)


def draw_prefix(key, part):
    key = jax.random.fold_in(key, 7)
    first_key, second_key = jax.random.split(key)
    lengths = jax.random.randint(first_key, (REQS,), PMAX // 4, PMAX + 1)
    chosen = jax.random.randint(second_key, (), 0, REQS)
    return lengths.at[chosen].set(PMAX).astype(jnp.int32)


def spiked(result, key, source, target, blocks, factor):
    def block_of(dim):
        return (jnp.arange(result.shape[dim]) // (result.shape[dim] // blocks)).reshape((-1,) + (1,) * (result.ndim - 1 - dim))

    first = jax.random.permutation(key, blocks)[block_of(target)]
    other_side = (block_of(target) + blocks // 2) % blocks
    return jnp.where((block_of(source) == first) | (block_of(source) == other_side), factor * result, result)


def steps_of(rng, shape, cuts, smallest, top_value):
    factor_of = 1.0
    for axis_at, shards_of in cuts:
        steps = jax.random.uniform(jax.random.fold_in(jax.random.fold_in(rng, 6), axis_at), (shards_of,), jnp.float32, smallest / len(cuts), top_value / len(cuts))
        factor_of = factor_of * jnp.repeat(jnp.exp(steps), shape[axis_at] // shards_of).reshape((-1,) + (1,) * (len(shape) - 1 - axis_at))
    return factor_of


def normal_values(own_key, shape, spread, reach, cuts=(), dtype=jnp.bfloat16):
    result = spread * jax.random.normal(own_key, shape, jnp.float32)
    if cuts:
        result = result * steps_of(own_key, shape, cuts, -0.22, 0.18)
    return jnp.clip(result, -reach, reach).astype(dtype)


def bell_draw_with(rng, dims, deviation, limit, shards, heavy, held_as=jnp.bfloat16):
    values = deviation * jax.random.normal(rng, dims, jnp.float32)
    if shards:
        values = values * steps_of(rng, dims, shards, -0.22, 0.18)
    return jnp.clip(spiked(values, jax.random.fold_in(rng, 3), *heavy), -limit, limit).astype(held_as)


def setup_inputs(seed: int = 0, part: int = 0) -> dict:
    key_list = jax.random.split(jax.random.key(seed), 6)
    own_keys = jax.random.split(jax.random.fold_in(key_list[5], part), 6)
    queries = draw_queries(jax.random.fold_in(jax.random.fold_in(key_list[5], part), 71), part)
    cache = draw_cache(jax.random.fold_in(jax.random.fold_in(key_list[5], part), 71), part)
    new_kv = normal_values(own_keys[2], (REQS, N_TP, 2, CH, HD), 1.0, 4.5, ((0, 4), (1, 4)))
    out_weight = bell_draw_with(key_list[3], (HQ * HD, DW), (HQ * HD) ** -0.5, 0.25, ((0, 4),), (0, 1, 4, 2.0))
    prefix = draw_prefix(jax.random.fold_in(jax.random.fold_in(key_list[5], part), 71), part)
    return {"queries": queries, "cache": cache, "new_kv": new_kv, "out_weight": out_weight, "prefix": prefix}


def encode(values):
    blocks = values.reshape(values.shape[:-1] + (values.shape[-1] // BLOCK, BLOCK))
    scales = (jnp.max(jnp.abs(blocks), axis=-1) + 1e-6).astype(jnp.bfloat16)
    encoded = (blocks / scales.astype(jnp.float32)[..., None]).astype(jnp.bfloat16)
    encoded, scales = lax.optimization_barrier((encoded, scales))
    return encoded.reshape(values.shape), scales


def decode(encoded, scales):
    blocks = encoded.reshape(encoded.shape[:-1] + (encoded.shape[-1] // BLOCK, BLOCK)).astype(jnp.float32)
    return (blocks * scales.astype(jnp.float32)[..., None]).reshape(encoded.shape)


def attend(query_rows, past_kv, fresh_kv, length):
    factor = HD ** -0.5
    query_heads = query_rows.reshape(CH, N_TP, HQ_DEV, HD).astype(jnp.float32)
    past_keys = past_kv[:, 0].astype(jnp.float32)
    past_values = past_kv[:, 1].astype(jnp.float32)
    fresh_keys = fresh_kv[:, 0].astype(jnp.float32)
    fresh_values = fresh_kv[:, 1].astype(jnp.float32)
    past_scores = jnp.einsum("cgkd,gpd->gkcp", query_heads, past_keys) * factor
    fresh_scores = jnp.einsum("cgkd,gjd->gkcj", query_heads, fresh_keys) * factor
    visible = jnp.arange(PMAX) < length
    causal = jnp.arange(CH)[None, :] <= jnp.arange(CH)[:, None]
    past_scores = jnp.where(visible, past_scores, -jnp.inf)
    fresh_scores = jnp.where(causal, fresh_scores, -jnp.inf)
    highest = jnp.maximum(jnp.max(past_scores, axis=-1), jnp.max(fresh_scores, axis=-1))[..., None]
    past_weights = jnp.exp(past_scores - highest)
    fresh_weights = jnp.exp(fresh_scores - highest)
    totals = jnp.sum(past_weights, axis=-1) + jnp.sum(fresh_weights, axis=-1)
    past_rounded, fresh_rounded = lax.optimization_barrier((past_weights.astype(jnp.bfloat16), fresh_weights.astype(jnp.bfloat16)))
    summed = jnp.einsum("gkcp,gpd->cgkd", past_rounded.astype(jnp.float32), past_values)
    summed = summed + jnp.einsum("gkcj,gjd->cgkd", fresh_rounded.astype(jnp.float32), fresh_values)
    attended = summed / jnp.transpose(totals, (2, 0, 1))[..., None]
    return attended.astype(jnp.bfloat16).reshape(CH, HQ * HD)


def reference(queries, cache, new_kv, out_weight, prefix):
    weights = out_weight.reshape(N_TP, HQ_DEV * HD, DW).astype(jnp.float32)

    def per_request(inputs):
        query_rows, past_kv, fresh_kv, length = inputs
        attended = attend(query_rows, past_kv, fresh_kv, length)
        partial_value = jnp.einsum("ctr,trd->tcd", attended.reshape(CH, N_TP, HQ_DEV * HD).astype(jnp.float32), weights)
        encoded, scales = encode(partial_value)
        summed = jnp.sum(decode(encoded, scales), axis=0)
        recoded, rescales = encode(summed)
        return decode(recoded, rescales).astype(jnp.bfloat16)

    return lax.map(per_request, (queries, cache, new_kv, prefix))
```

```python
import functools
import math

import jax
import jax.numpy as jnp
from jax import lax
from jax.experimental import pallas as pl
from jax.experimental.pallas import tpu as pltpu
from jax.sharding import PartitionSpec as P

HD = 128
HQ_DEV = 2
CH = 128
SAFE = 896
TILE = 512
CHUNK = 256
LAG = 4
MASKED = -1e30
MESH = pl.DeviceIdType.MESH
NT = (((1,), (1,)), ((), ()))


def kernel(n, q_ref, cache_ref, new_ref, w_hbm, prefix_ref, out_ref,
           kv, weight, scores, attended, stage, landed,
           load_sem, rs_send, rs_recv, ag_send, ag_recv):
    t = lax.axis_index("tp")
    pmax = cache_ref.shape[1]
    dw = w_hbm.shape[1]
    half = dw // 2
    count = half // CHUNK
    has_prev = t > 0
    has_next = t < n - 1
    prev, nxt = jnp.maximum(t - 1, 0), jnp.minimum(t + 1, n - 1)

    loads = [
        pltpu.make_async_copy(cache_ref.at[0], kv.at[0], load_sem.at[0]),
        pltpu.make_async_copy(cache_ref.at[1], kv.at[1], load_sem.at[1]),
        pltpu.make_async_copy(w_hbm, weight, load_sem.at[2]),
    ]
    for load in loads:
        load.start()

    barrier = pltpu.get_barrier_semaphore()

    @pl.when(has_prev)
    def _():
        pl.semaphore_signal(barrier, inc=1, device_id={"tp": prev}, device_id_type=MESH)

    @pl.when(has_next)
    def _():
        pl.semaphore_signal(barrier, inc=1, device_id={"tp": nxt}, device_id_type=MESH)

    factor = HD ** -0.5 * math.log2(math.e)
    length = prefix_ref[0]
    rows = HQ_DEV * CH
    query = jnp.concatenate([q_ref[:, h * HD:(h + 1) * HD] for h in range(HQ_DEV)], axis=0)
    top = jnp.full((rows, 128), MASKED, jnp.float32)

    def widest(top, tile):
        for j in range(tile.shape[1] // 128):
            top = jnp.maximum(top, tile[:, j * 128:(j + 1) * 128])
        return top

    row = lax.broadcasted_iota(jnp.int32, (rows, CH), 0) % CH
    col = lax.broadcasted_iota(jnp.int32, (rows, CH), 1)
    fresh = lax.dot_general(query, new_ref[0], NT, preferred_element_type=jnp.float32)
    fresh = jnp.where(col <= row, fresh, MASKED)
    top = widest(top, fresh)
    loads[0].wait()
    for start in range(0, pmax, TILE):
        size = min(TILE, pmax - start)
        tile = lax.dot_general(query, kv[0, start:start + size], NT, preferred_element_type=jnp.float32)
        if start + size > SAFE:
            slot = lax.broadcasted_iota(jnp.int32, (1, size), 1) + start
            tile = jnp.where(slot < length, tile, MASKED)
        scores[:, start:start + size] = tile
        top = widest(top, tile)
    highest = jnp.max(top, axis=1, keepdims=True) * factor

    def weigh(tile, total):
        weights = jnp.exp2(tile * factor - highest)
        for j in range(tile.shape[1] // 128):
            total = total + weights[:, j * 128:(j + 1) * 128]
        return weights.astype(jnp.bfloat16), total

    total = jnp.zeros((rows, 128), jnp.float32)
    weights, total = weigh(fresh, total)
    summed = jnp.dot(weights, new_ref[1], preferred_element_type=jnp.float32)
    loads[1].wait()
    for start in range(0, pmax, TILE):
        size = min(TILE, pmax - start)
        weights, total = weigh(scores[:, start:start + size], total)
        summed = summed + jnp.dot(weights, kv[1, start:start + size], preferred_element_type=jnp.float32)
    summed = summed / jnp.sum(total, axis=1, keepdims=True)
    for h in range(HQ_DEV):
        attended[:, h * HD:(h + 1) * HD] = summed[h * CH:(h + 1) * CH].astype(jnp.bfloat16)

    loads[2].wait()
    pl.semaphore_wait(barrier, has_prev.astype(jnp.int32) + has_next.astype(jnp.int32))

    towards = (nxt, prev)
    back = (prev, nxt)
    is_first = (t == 0, t == n - 1)
    is_owner = (t == n - 1, t == 0)

    def columns(d, i):
        return pl.ds(pl.multiple_of((1 - d) * half + i * CHUNK, CHUNK), CHUNK)

    def sum_copy(d, i):
        return pltpu.make_async_remote_copy(
            src_ref=stage.at[d, i], dst_ref=landed.at[d, i],
            send_sem=rs_send.at[d, i], recv_sem=rs_recv.at[d, i],
            device_id={"tp": towards[d]}, device_id_type=MESH)

    def result_copy(d, i):
        return pltpu.make_async_remote_copy(
            src_ref=out_ref.at[:, columns(d, i)], dst_ref=out_ref.at[:, columns(d, i)],
            send_sem=ag_send.at[d, i], recv_sem=ag_recv.at[d, i],
            device_id={"tp": back[d]}, device_id_type=MESH)

    def sum_step(d, i):
        part = jnp.dot(attended[...], weight[:, columns(d, i)], preferred_element_type=jnp.float32)

        @pl.when(is_first[d])
        def _():
            stage[d, i] = part.astype(jnp.bfloat16)
            sum_copy(d, i).start()

        @pl.when(jnp.logical_not(is_first[d]))
        def _():
            sum_copy(d, i).wait_recv()
            running = (part + landed[d, i].astype(jnp.float32)).astype(jnp.bfloat16)

            @pl.when(is_owner[d])
            def _():
                out_ref[:, columns(d, i)] = running
                result_copy(d, i).start()

            @pl.when(jnp.logical_not(is_owner[d]))
            def _():
                stage[d, i] = running
                sum_copy(d, i).start()

    def result_step(d, i):
        @pl.when(jnp.logical_not(is_owner[d]))
        def _():
            result_copy(d, i).wait_recv()

            @pl.when(jnp.logical_not(is_first[d]))
            def _():
                result_copy(d, i).start()

    lag = min(LAG, count)

    @pl.loop(0, lag)
    def _(i):
        for d in range(2):
            sum_step(d, i)

    @pl.loop(lag, count)
    def _(i):
        for d in range(2):
            sum_step(d, i)
        for d in range(2):
            result_step(d, i - lag)

    @pl.loop(count - lag, count)
    def _(i):
        for d in range(2):
            result_step(d, i)

    @pl.loop(0, count)
    def _(i):
        for d in range(2):
            @pl.when(jnp.logical_not(is_owner[d]))
            def _():
                sum_copy(d, i).wait_send()

            @pl.when(jnp.logical_not(is_first[d]))
            def _():
                result_copy(d, i).wait_send()


def per_device(queries, cache, new_kv, out_weight, prefix):
    n = lax.axis_size("tp")
    pmax = cache.shape[3]
    dw = out_weight.shape[1]
    count = dw // 2 // CHUNK
    vmem = pl.BlockSpec(memory_space=pltpu.VMEM)
    hbm = pl.BlockSpec(memory_space=pl.ANY)
    out = pl.pallas_call(
        functools.partial(kernel, n),
        out_shape=jax.ShapeDtypeStruct((CH, dw), jnp.bfloat16),
        in_specs=[vmem, hbm, vmem, hbm, pl.BlockSpec(memory_space=pltpu.SMEM)],
        out_specs=vmem,
        scratch_shapes=[
            pltpu.VMEM((2, pmax, HD), jnp.bfloat16),
            pltpu.VMEM(out_weight.shape, jnp.bfloat16),
            pltpu.VMEM((HQ_DEV * CH, pmax), jnp.float32),
            pltpu.VMEM((CH, HQ_DEV * HD), jnp.bfloat16),
            pltpu.VMEM((2, count, CH, CHUNK), jnp.bfloat16),
            pltpu.VMEM((2, count, CH, CHUNK), jnp.bfloat16),
            pltpu.SemaphoreType.DMA((3,)),
            pltpu.SemaphoreType.DMA((2, count)),
            pltpu.SemaphoreType.DMA((2, count)),
            pltpu.SemaphoreType.DMA((2, count)),
            pltpu.SemaphoreType.DMA((2, count)),
        ],
        compiler_params=pltpu.CompilerParams(
            collective_id=0, has_side_effects=True, vmem_limit_bytes=48 * 1024 * 1024),
    )(queries[0], cache[0, 0], new_kv[0, 0], out_weight, prefix)
    return out[None]


def solution(mesh):
    in_specs = (
        P(("groups", "dp"), None, "tp"),
        P(("groups", "dp"), "tp", None, None, None),
        P(("groups", "dp"), "tp", None, None, None),
        P("tp", None),
        P(("groups", "dp")),
    )
    out_specs = P(("groups", "dp"), None, None)
    return jax.shard_map(
        per_device, mesh=mesh, in_specs=in_specs, out_specs=out_specs, check_vma=False
    )
```

```python
import functools
import math

import jax
import jax.numpy as jnp
from jax import lax
from jax.experimental import pallas as pl
from jax.experimental.pallas import tpu as pltpu
from jax.sharding import PartitionSpec as P

HD = 128
HQ_DEV = 2
CH = 128
SAFE = 896
TILE = 512
CHUNK = 256
SKEW = 2
MASKED = -1e30
MESH = pl.DeviceIdType.MESH
NT = (((1,), (1,)), ((), ()))


def kernel(n, q_ref, cache_ref, new_ref, w_hbm, prefix_ref, out_ref,
           query2, fresh_kv, kv, weight, scores, attended, stage, landed,
           results, load_sem, rs_send, rs_recv, ag_send, ag_recv):
    t = lax.axis_index("tp")
    pmax = cache_ref.shape[1]
    dw = w_hbm.shape[1]
    half = dw // 2
    count = half // CHUNK
    has_prev = t > 0
    has_next = t < n - 1
    prev, nxt = jnp.maximum(t - 1, 0), jnp.minimum(t + 1, n - 1)

    loads = [
        pltpu.make_async_copy(q_ref, query2, load_sem.at[3]),
        pltpu.make_async_copy(new_ref, fresh_kv, load_sem.at[4]),
        pltpu.make_async_copy(cache_ref.at[0], kv.at[0], load_sem.at[0]),
        pltpu.make_async_copy(cache_ref.at[1], kv.at[1], load_sem.at[1]),
        pltpu.make_async_copy(w_hbm, weight, load_sem.at[2]),
    ]
    for load in loads:
        load.start()

    barrier = pltpu.get_barrier_semaphore()

    @pl.when(has_prev)
    def _():
        pl.semaphore_signal(barrier, inc=1, device_id={"tp": prev}, device_id_type=MESH)

    @pl.when(has_next)
    def _():
        pl.semaphore_signal(barrier, inc=1, device_id={"tp": nxt}, device_id_type=MESH)

    factor = HD ** -0.5 * math.log2(math.e)
    length = prefix_ref[0]
    rows = HQ_DEV * CH
    loads[0].wait()
    loads[1].wait()
    query = jnp.concatenate([query2[:, h * HD:(h + 1) * HD] for h in range(HQ_DEV)], axis=0)
    top = jnp.full((rows, 128), MASKED, jnp.float32)

    def widest(top, tile):
        for j in range(tile.shape[1] // 128):
            top = jnp.maximum(top, tile[:, j * 128:(j + 1) * 128])
        return top

    row = lax.broadcasted_iota(jnp.int32, (rows, CH), 0) % CH
    col = lax.broadcasted_iota(jnp.int32, (rows, CH), 1)
    fresh = lax.dot_general(query, fresh_kv[0], NT, preferred_element_type=jnp.float32)
    fresh = jnp.where(col <= row, fresh, MASKED)
    top = widest(top, fresh)
    loads[2].wait()
    for start in range(0, pmax, TILE):
        size = min(TILE, pmax - start)
        tile = lax.dot_general(query, kv[0, start:start + size], NT, preferred_element_type=jnp.float32)
        if start + size > SAFE:
            slot = lax.broadcasted_iota(jnp.int32, (1, size), 1) + start
            tile = jnp.where(slot < length, tile, MASKED)
        scores[:, start:start + size] = tile
        top = widest(top, tile)
    highest = jnp.max(top, axis=1, keepdims=True) * factor

    def weigh(tile, total):
        weights = jnp.exp2(tile * factor - highest)
        for j in range(tile.shape[1] // 128):
            total = total + weights[:, j * 128:(j + 1) * 128]
        return weights.astype(jnp.bfloat16), total

    total = jnp.zeros((rows, 128), jnp.float32)
    weights, total = weigh(fresh, total)
    summed = jnp.dot(weights, fresh_kv[1], preferred_element_type=jnp.float32)
    loads[3].wait()
    for start in range(0, pmax, TILE):
        size = min(TILE, pmax - start)
        weights, total = weigh(scores[:, start:start + size], total)
        summed = summed + jnp.dot(weights, kv[1, start:start + size], preferred_element_type=jnp.float32)
    summed = summed / jnp.sum(total, axis=1, keepdims=True)
    for h in range(HQ_DEV):
        attended[:, h * HD:(h + 1) * HD] = summed[h * CH:(h + 1) * CH].astype(jnp.bfloat16)

    loads[4].wait()
    pl.semaphore_wait(barrier, has_prev.astype(jnp.int32) + has_next.astype(jnp.int32))

    towards = (nxt, prev)
    back = (prev, nxt)
    is_first = (t == 0, t == n - 1)
    is_owner = (t == n - 1, t == 0)

    def columns(d, i):
        return pl.ds(pl.multiple_of((1 - d) * half + i * CHUNK, CHUNK), CHUNK)

    def sum_copy(d, i):
        return pltpu.make_async_remote_copy(
            src_ref=stage.at[d, i], dst_ref=landed.at[d, i],
            send_sem=rs_send.at[d, i], recv_sem=rs_recv.at[d, i],
            device_id={"tp": towards[d]}, device_id_type=MESH)

    def result_copy(d, i):
        return pltpu.make_async_remote_copy(
            src_ref=results.at[d, i], dst_ref=results.at[d, i],
            send_sem=ag_send.at[d, i], recv_sem=ag_recv.at[d, i],
            device_id={"tp": back[d]}, device_id_type=MESH)

    def sum_step(d, i):
        part = jnp.dot(attended[...], weight[:, columns(d, i)], preferred_element_type=jnp.float32)

        @pl.when(is_first[d])
        def _():
            stage[d, i] = part.astype(jnp.bfloat16)
            sum_copy(d, i).start()

        @pl.when(jnp.logical_not(is_first[d]))
        def _():
            sum_copy(d, i).wait_recv()
            running = (part + landed[d, i].astype(jnp.float32)).astype(jnp.bfloat16)

            @pl.when(is_owner[d])
            def _():
                results[d, i] = running
                out_ref[:, columns(d, i)] = running
                result_copy(d, i).start()

            @pl.when(jnp.logical_not(is_owner[d]))
            def _():
                stage[d, i] = running
                sum_copy(d, i).start()

    def result_step(d, i):
        @pl.when(jnp.logical_not(is_owner[d]))
        def _():
            result_copy(d, i).wait_recv()

            @pl.when(jnp.logical_not(is_first[d]))
            def _():
                result_copy(d, i).start()

            out_ref[:, columns(d, i)] = results[d, i]

    far = n - 1
    hops = ((t, far - t), (far + far - t, far + t))

    @pl.loop(0, count + 2 * far * SKEW)
    def _(step):
        for delays, work in zip(hops, (sum_step, result_step)):
            for d in range(2):
                i = step - delays[d] * SKEW

                @pl.when((i >= 0) & (i < count))
                def _():
                    work(d, i)

    @pl.loop(0, count)
    def _(i):
        for d in range(2):
            @pl.when(jnp.logical_not(is_owner[d]))
            def _():
                sum_copy(d, i).wait_send()

            @pl.when(jnp.logical_not(is_first[d]))
            def _():
                result_copy(d, i).wait_send()


def per_device(queries, cache, new_kv, out_weight, prefix):
    n = lax.axis_size("tp")
    pmax = cache.shape[3]
    dw = out_weight.shape[1]
    count = dw // 2 // CHUNK
    vmem = pl.BlockSpec(memory_space=pltpu.VMEM)
    hbm = pl.BlockSpec(memory_space=pltpu.HBM)
    out = pl.pallas_call(
        functools.partial(kernel, n),
        out_shape=jax.ShapeDtypeStruct((CH, dw), jnp.bfloat16),
        in_specs=[hbm, hbm, hbm, hbm, pl.BlockSpec(memory_space=pltpu.SMEM)],
        out_specs=vmem,
        scratch_shapes=[
            pltpu.VMEM((CH, HQ_DEV * HD), jnp.bfloat16),
            pltpu.VMEM((2, CH, HD), jnp.bfloat16),
            pltpu.VMEM((2, pmax, HD), jnp.bfloat16),
            pltpu.VMEM(out_weight.shape, jnp.bfloat16),
            pltpu.VMEM((HQ_DEV * CH, pmax), jnp.float32),
            pltpu.VMEM((CH, HQ_DEV * HD), jnp.bfloat16),
            pltpu.VMEM((2, count, CH, CHUNK), jnp.bfloat16),
            pltpu.VMEM((2, count, CH, CHUNK), jnp.bfloat16),
            pltpu.VMEM((2, count, CH, CHUNK), jnp.bfloat16),
            pltpu.SemaphoreType.DMA((5,)),
            pltpu.SemaphoreType.DMA((2, count)),
            pltpu.SemaphoreType.DMA((2, count)),
            pltpu.SemaphoreType.DMA((2, count)),
            pltpu.SemaphoreType.DMA((2, count)),
        ],
        compiler_params=pltpu.CompilerParams(
            collective_id=0, has_side_effects=True, vmem_limit_bytes=48 * 1024 * 1024),
    )(queries[0], cache[0, 0], new_kv[0, 0], out_weight, prefix)
    return out[None]


def solution(mesh):
    in_specs = (
        P(("groups", "dp"), None, "tp"),
        P(("groups", "dp"), "tp", None, None, None),
        P(("groups", "dp"), "tp", None, None, None),
        P("tp", None),
        P(("groups", "dp")),
    )
    out_specs = P(("groups", "dp"), None, None)
    return jax.shard_map(
        per_device, mesh=mesh, in_specs=in_specs, out_specs=out_specs, check_vma=False
    )
```

```python
import functools
import math

import jax
import jax.numpy as jnp
from jax import lax
from jax.experimental import pallas as pl
from jax.experimental.pallas import tpu as pltpu
from jax.sharding import PartitionSpec as P

HD = 128
HQ_DEV = 2
CH = 128
SAFE = 896
TILE = 512
CHUNK = 128
SKEW = 5
MASKED = -1e30
MESH = pl.DeviceIdType.MESH
NT = (((1,), (1,)), ((), ()))


def kernel(n, q_ref, cache_ref, new_ref, w_hbm, prefix_ref, out_ref,
           query2, fresh_kv, kv, weight, scores, attended, parts, stage, landed,
           results, load_sem, rs_send, rs_recv, ag_send, ag_recv):
    t = lax.axis_index("tp")
    pmax = cache_ref.shape[1]
    dw = w_hbm.shape[1]
    half = dw // 2
    count = half // CHUNK
    has_prev = t > 0
    has_next = t < n - 1
    prev, nxt = jnp.maximum(t - 1, 0), jnp.minimum(t + 1, n - 1)

    loads = [
        pltpu.make_async_copy(q_ref, query2, load_sem.at[3]),
        pltpu.make_async_copy(new_ref, fresh_kv, load_sem.at[4]),
        pltpu.make_async_copy(cache_ref.at[0], kv.at[0], load_sem.at[0]),
        pltpu.make_async_copy(cache_ref.at[1], kv.at[1], load_sem.at[1]),
        pltpu.make_async_copy(w_hbm, weight, load_sem.at[2]),
    ]
    for load in loads:
        load.start()

    barrier = pltpu.get_barrier_semaphore()

    @pl.when(has_prev)
    def _():
        pl.semaphore_signal(barrier, inc=1, device_id={"tp": prev}, device_id_type=MESH)

    @pl.when(has_next)
    def _():
        pl.semaphore_signal(barrier, inc=1, device_id={"tp": nxt}, device_id_type=MESH)

    factor = HD ** -0.5 * math.log2(math.e)
    length = prefix_ref[0]
    rows = HQ_DEV * CH
    loads[0].wait()
    loads[1].wait()
    query = jnp.concatenate([query2[:, h * HD:(h + 1) * HD] for h in range(HQ_DEV)], axis=0)
    top = jnp.full((rows, 128), MASKED, jnp.float32)

    def widest(top, tile):
        for j in range(tile.shape[1] // 128):
            top = jnp.maximum(top, tile[:, j * 128:(j + 1) * 128])
        return top

    row = lax.broadcasted_iota(jnp.int32, (rows, CH), 0) % CH
    col = lax.broadcasted_iota(jnp.int32, (rows, CH), 1)
    fresh = lax.dot_general(query, fresh_kv[0], NT, preferred_element_type=jnp.float32)
    fresh = jnp.where(col <= row, fresh, MASKED)
    top = widest(top, fresh)
    loads[2].wait()
    for start in range(0, pmax, TILE):
        size = min(TILE, pmax - start)
        tile = lax.dot_general(query, kv[0, start:start + size], NT, preferred_element_type=jnp.float32)
        if start + size > SAFE:
            slot = lax.broadcasted_iota(jnp.int32, (1, size), 1) + start
            tile = jnp.where(slot < length, tile, MASKED)
        scores[:, start:start + size] = tile
        top = widest(top, tile)
    highest = jnp.max(top, axis=1, keepdims=True) * factor

    def weigh(tile, total):
        weights = jnp.exp2(tile * factor - highest)
        for j in range(tile.shape[1] // 128):
            total = total + weights[:, j * 128:(j + 1) * 128]
        return weights.astype(jnp.bfloat16), total

    total = jnp.zeros((rows, 128), jnp.float32)
    weights, total = weigh(fresh, total)
    summed = jnp.dot(weights, fresh_kv[1], preferred_element_type=jnp.float32)
    loads[3].wait()
    for start in range(0, pmax, TILE):
        size = min(TILE, pmax - start)
        weights, total = weigh(scores[:, start:start + size], total)
        summed = summed + jnp.dot(weights, kv[1, start:start + size], preferred_element_type=jnp.float32)
    summed = summed / jnp.sum(total, axis=1, keepdims=True)
    for h in range(HQ_DEV):
        attended[:, h * HD:(h + 1) * HD] = summed[h * CH:(h + 1) * CH].astype(jnp.bfloat16)

    loads[4].wait()
    pl.semaphore_wait(barrier, has_prev.astype(jnp.int32) + has_next.astype(jnp.int32))

    towards = (nxt, prev)
    back = (prev, nxt)
    is_first = (t == 0, t == n - 1)
    is_owner = (t == n - 1, t == 0)

    def columns(d, i):
        return pl.ds(pl.multiple_of((1 - d) * half + i * CHUNK, CHUNK), CHUNK)

    def sum_copy(d, i):
        return pltpu.make_async_remote_copy(
            src_ref=stage.at[d, i], dst_ref=landed.at[d, i],
            send_sem=rs_send.at[d, i], recv_sem=rs_recv.at[d, i],
            device_id={"tp": towards[d]}, device_id_type=MESH)

    def result_copy(d, i):
        return pltpu.make_async_remote_copy(
            src_ref=results.at[d, i], dst_ref=results.at[d, i],
            send_sem=ag_send.at[d, i], recv_sem=ag_recv.at[d, i],
            device_id={"tp": back[d]}, device_id_type=MESH)

    def project(d, i):
        parts[d, i] = jnp.dot(attended[...], weight[:, columns(d, i)], preferred_element_type=jnp.float32)

    def sum_step(d, i):
        part = parts[d, i]

        @pl.when(is_first[d])
        def _():
            stage[d, i] = part.astype(jnp.bfloat16)
            sum_copy(d, i).start()

        @pl.when(jnp.logical_not(is_first[d]))
        def _():
            sum_copy(d, i).wait_recv()
            running = (part + landed[d, i].astype(jnp.float32)).astype(jnp.bfloat16)

            @pl.when(is_owner[d])
            def _():
                results[d, i] = running
                out_ref[:, columns(d, i)] = running

            @pl.when(jnp.logical_not(is_owner[d]))
            def _():
                stage[d, i] = running
                sum_copy(d, i).start()

    def result_step(d, i):
        @pl.when(is_owner[d])
        def _():
            result_copy(d, i).start()

        @pl.when(jnp.logical_not(is_owner[d]))
        def _():
            result_copy(d, i).wait_recv()

            @pl.when(jnp.logical_not(is_first[d]))
            def _():
                result_copy(d, i).start()

            out_ref[:, columns(d, i)] = results[d, i]

    far = n - 1
    turn = max(count, far * SKEW)
    hops = (t * SKEW, (far - t) * SKEW)

    @pl.loop(-1, turn + count + far * SKEW)
    def _(step):
        for work, delays in (
            (sum_step, hops),
            (result_step, (turn + hops[1], turn + hops[0])),
            (project, (hops[0] - 1, hops[1] - 1)),
        ):
            for d in range(2):
                i = step - delays[d]

                @pl.when((i >= 0) & (i < count))
                def _():
                    work(d, i)

    @pl.loop(0, count)
    def _(i):
        for d in range(2):
            @pl.when(jnp.logical_not(is_owner[d]))
            def _():
                sum_copy(d, i).wait_send()

            @pl.when(jnp.logical_not(is_first[d]))
            def _():
                result_copy(d, i).wait_send()


def per_device(queries, cache, new_kv, out_weight, prefix):
    n = lax.axis_size("tp")
    pmax = cache.shape[3]
    dw = out_weight.shape[1]
    count = dw // 2 // CHUNK
    vmem = pl.BlockSpec(memory_space=pltpu.VMEM)
    hbm = pl.BlockSpec(memory_space=pltpu.HBM)
    out = pl.pallas_call(
        functools.partial(kernel, n),
        out_shape=jax.ShapeDtypeStruct((CH, dw), jnp.bfloat16),
        in_specs=[hbm, hbm, hbm, hbm, pl.BlockSpec(memory_space=pltpu.SMEM)],
        out_specs=vmem,
        scratch_shapes=[
            pltpu.VMEM((CH, HQ_DEV * HD), jnp.bfloat16),
            pltpu.VMEM((2, CH, HD), jnp.bfloat16),
            pltpu.VMEM((2, pmax, HD), jnp.bfloat16),
            pltpu.VMEM(out_weight.shape, jnp.bfloat16),
            pltpu.VMEM((HQ_DEV * CH, pmax), jnp.float32),
            pltpu.VMEM((CH, HQ_DEV * HD), jnp.bfloat16),
            pltpu.VMEM((2, count, CH, CHUNK), jnp.float32),
            pltpu.VMEM((2, count, CH, CHUNK), jnp.bfloat16),
            pltpu.VMEM((2, count, CH, CHUNK), jnp.bfloat16),
            pltpu.VMEM((2, count, CH, CHUNK), jnp.bfloat16),
            pltpu.SemaphoreType.DMA((5,)),
            pltpu.SemaphoreType.DMA((2, count)),
            pltpu.SemaphoreType.DMA((2, count)),
            pltpu.SemaphoreType.DMA((2, count)),
            pltpu.SemaphoreType.DMA((2, count)),
        ],
        compiler_params=pltpu.CompilerParams(
            collective_id=0, has_side_effects=True, vmem_limit_bytes=63 * 1024 * 1024),
    )(queries[0], cache[0, 0], new_kv[0, 0], out_weight, prefix)
    return out[None]


def solution(mesh):
    in_specs = (
        P(("groups", "dp"), None, "tp"),
        P(("groups", "dp"), "tp", None, None, None),
        P(("groups", "dp"), "tp", None, None, None),
        P("tp", None),
        P(("groups", "dp")),
    )
    out_specs = P(("groups", "dp"), None, None)
    return jax.shard_map(
        per_device, mesh=mesh, in_specs=in_specs, out_specs=out_specs, check_vma=False
    )
```

```python
import functools
import math

import jax
import jax.numpy as jnp
from jax import lax
from jax.experimental import pallas as pl
from jax.experimental.pallas import tpu as pltpu
from jax.sharding import PartitionSpec as P

HD = 128
HQ_DEV = 2
CH = 128
SAFE = 896
TILE = 512
WIDE = 256
PARTS = 2
SKEW = 5
MASKED = -1e30
MESH = pl.DeviceIdType.MESH
NT = (((1,), (1,)), ((), ()))


def kernel(n, q_ref, cache_ref, new_ref, w_hbm, prefix_ref, out_ref,
           query2, fresh_kv, kv, weight, scores, attended, parts, stage, landed,
           results, load_sem, rs_send, rs_recv, ag_send, ag_recv):
    t = lax.axis_index("tp")
    pmax = cache_ref.shape[1]
    dw = w_hbm.shape[1]
    half = dw // 2
    per_part = half // WIDE
    count = PARTS * per_part
    deep = CH // PARTS
    has_prev = t > 0
    has_next = t < n - 1
    prev, nxt = jnp.maximum(t - 1, 0), jnp.minimum(t + 1, n - 1)

    loads = [
        pltpu.make_async_copy(q_ref, query2, load_sem.at[3]),
        pltpu.make_async_copy(new_ref, fresh_kv, load_sem.at[4]),
        pltpu.make_async_copy(cache_ref.at[0], kv.at[0], load_sem.at[0]),
        pltpu.make_async_copy(cache_ref.at[1], kv.at[1], load_sem.at[1]),
        pltpu.make_async_copy(w_hbm, weight, load_sem.at[2]),
    ]
    for load in loads:
        load.start()

    barrier = pltpu.get_barrier_semaphore()

    @pl.when(has_prev)
    def _():
        pl.semaphore_signal(barrier, inc=1, device_id={"tp": prev}, device_id_type=MESH)

    @pl.when(has_next)
    def _():
        pl.semaphore_signal(barrier, inc=1, device_id={"tp": nxt}, device_id_type=MESH)

    factor = HD ** -0.5 * math.log2(math.e)
    length = prefix_ref[0]
    rows = HQ_DEV * deep

    def widest(top, tile):
        for j in range(tile.shape[1] // 128):
            top = jnp.maximum(top, tile[:, j * 128:(j + 1) * 128])
        return top

    def attend(part):
        mine = slice(part * deep, (part + 1) * deep)
        query = jnp.concatenate([query2[mine, h * HD:(h + 1) * HD] for h in range(HQ_DEV)], axis=0)
        top = jnp.full((rows, 128), MASKED, jnp.float32)
        row = lax.broadcasted_iota(jnp.int32, (rows, CH), 0) % deep + part * deep
        col = lax.broadcasted_iota(jnp.int32, (rows, CH), 1)
        fresh = lax.dot_general(query, fresh_kv[0], NT, preferred_element_type=jnp.float32)
        fresh = jnp.where(col <= row, fresh, MASKED)
        top = widest(top, fresh)
        if part == 0:
            loads[2].wait()
        for start in range(0, pmax, TILE):
            size = min(TILE, pmax - start)
            tile = lax.dot_general(query, kv[0, start:start + size], NT, preferred_element_type=jnp.float32)
            if start + size > SAFE:
                slot = lax.broadcasted_iota(jnp.int32, (1, size), 1) + start
                tile = jnp.where(slot < length, tile, MASKED)
            scores[:, start:start + size] = tile
            top = widest(top, tile)
        highest = jnp.max(top, axis=1, keepdims=True) * factor

        def weigh(tile, total):
            weights = jnp.exp2(tile * factor - highest)
            for j in range(tile.shape[1] // 128):
                total = total + weights[:, j * 128:(j + 1) * 128]
            return weights.astype(jnp.bfloat16), total

        total = jnp.zeros((rows, 128), jnp.float32)
        weights, total = weigh(fresh, total)
        summed = jnp.dot(weights, fresh_kv[1], preferred_element_type=jnp.float32)
        if part == 0:
            loads[3].wait()
        for start in range(0, pmax, TILE):
            size = min(TILE, pmax - start)
            weights, total = weigh(scores[:, start:start + size], total)
            summed = summed + jnp.dot(weights, kv[1, start:start + size], preferred_element_type=jnp.float32)
        summed = summed / jnp.sum(total, axis=1, keepdims=True)
        for h in range(HQ_DEV):
            attended[mine, h * HD:(h + 1) * HD] = summed[h * deep:(h + 1) * deep].astype(jnp.bfloat16)

    loads[0].wait()
    loads[1].wait()

    towards = (nxt, prev)
    back = (prev, nxt)
    is_first = (t == 0, t == n - 1)
    is_owner = (t == n - 1, t == 0)

    def tokens(i):
        return pl.ds(pl.multiple_of(i // per_part * deep, deep), deep)

    def columns(d, i):
        return pl.ds(pl.multiple_of((1 - d) * half + i % per_part * WIDE, WIDE), WIDE)

    def sum_copy(d, i):
        return pltpu.make_async_remote_copy(
            src_ref=stage.at[d, i], dst_ref=landed.at[d, i],
            send_sem=rs_send.at[d, i], recv_sem=rs_recv.at[d, i],
            device_id={"tp": towards[d]}, device_id_type=MESH)

    def result_copy(d, i):
        return pltpu.make_async_remote_copy(
            src_ref=results.at[d, i], dst_ref=results.at[d, i],
            send_sem=ag_send.at[d, i], recv_sem=ag_recv.at[d, i],
            device_id={"tp": back[d]}, device_id_type=MESH)

    early = count - per_part

    def project(d, i):
        @pl.when(jnp.logical_not(is_first[d]) | (i >= early))
        def _():
            parts[d, i] = product(d, i)

    def product(d, i):
        return jnp.dot(attended[tokens(i), :], weight[:, columns(d, i)], preferred_element_type=jnp.float32)

    def sum_step(d, i):
        part = parts[d, i]

        @pl.when(is_first[d] & (i >= early))
        def _():
            stage[d, i] = part.astype(jnp.bfloat16)
            sum_copy(d, i).start()

        @pl.when(jnp.logical_not(is_first[d]))
        def _():
            sum_copy(d, i).wait_recv()
            running = (part + landed[d, i].astype(jnp.float32)).astype(jnp.bfloat16)

            @pl.when(is_owner[d])
            def _():
                results[d, i] = running
                out_ref[tokens(i), columns(d, i)] = running

            @pl.when(jnp.logical_not(is_owner[d]))
            def _():
                stage[d, i] = running
                sum_copy(d, i).start()

    def result_step(d, i):
        @pl.when(is_owner[d])
        def _():
            result_copy(d, i).start()

        @pl.when(jnp.logical_not(is_owner[d]))
        def _():
            result_copy(d, i).wait_recv()

            @pl.when(jnp.logical_not(is_first[d]))
            def _():
                result_copy(d, i).start()

            out_ref[tokens(i), columns(d, i)] = results[d, i]

    for part in range(PARTS):
        attend(part)
        if part == 0:
            loads[4].wait()
            pl.semaphore_wait(barrier, has_prev.astype(jnp.int32) + has_next.astype(jnp.int32))
        if part < PARTS - 1:
            for d in range(2):
                @pl.when(is_first[d])
                def _():
                    @pl.loop(part * per_part, (part + 1) * per_part)
                    def _(i):
                        stage[d, i] = product(d, i).astype(jnp.bfloat16)
                        sum_copy(d, i).start()

    far = n - 1
    turn = max(count, far * SKEW)
    hops = (t * SKEW, (far - t) * SKEW)

    @pl.loop(-1, turn + count + far * SKEW)
    def _(step):
        for work, delays in (
            (sum_step, hops),
            (result_step, (turn + hops[1], turn + hops[0])),
            (project, (hops[0] - 1, hops[1] - 1)),
        ):
            for d in range(2):
                i = step - delays[d]

                @pl.when((i >= 0) & (i < count))
                def _():
                    work(d, i)

    @pl.loop(0, count)
    def _(i):
        for d in range(2):
            @pl.when(jnp.logical_not(is_owner[d]))
            def _():
                sum_copy(d, i).wait_send()

            @pl.when(jnp.logical_not(is_first[d]))
            def _():
                result_copy(d, i).wait_send()


def per_device(queries, cache, new_kv, out_weight, prefix):
    n = lax.axis_size("tp")
    pmax = cache.shape[3]
    dw = out_weight.shape[1]
    count = PARTS * (dw // 2 // WIDE)
    deep = CH // PARTS
    vmem = pl.BlockSpec(memory_space=pltpu.VMEM)
    hbm = pl.BlockSpec(memory_space=pltpu.HBM)
    out = pl.pallas_call(
        functools.partial(kernel, n),
        out_shape=pltpu.VMEM((CH, dw), jnp.bfloat16),
        in_specs=[hbm, hbm, hbm, hbm, pl.BlockSpec(memory_space=pltpu.SMEM)],
        out_specs=vmem,
        scratch_shapes=[
            pltpu.VMEM((CH, HQ_DEV * HD), jnp.bfloat16),
            pltpu.VMEM((2, CH, HD), jnp.bfloat16),
            pltpu.VMEM((2, pmax, HD), jnp.bfloat16),
            pltpu.VMEM(out_weight.shape, jnp.bfloat16),
            pltpu.VMEM((HQ_DEV * deep, pmax), jnp.float32),
            pltpu.VMEM((CH, HQ_DEV * HD), jnp.bfloat16),
            pltpu.VMEM((2, count, deep, WIDE), jnp.float32),
            pltpu.VMEM((2, count, deep, WIDE), jnp.bfloat16),
            pltpu.VMEM((2, count, deep, WIDE), jnp.bfloat16),
            pltpu.VMEM((2, count, deep, WIDE), jnp.bfloat16),
            pltpu.SemaphoreType.DMA((5,)),
            pltpu.SemaphoreType.DMA((2, count)),
            pltpu.SemaphoreType.DMA((2, count)),
            pltpu.SemaphoreType.DMA((2, count)),
            pltpu.SemaphoreType.DMA((2, count)),
        ],
        compiler_params=pltpu.CompilerParams(
            collective_id=0, has_side_effects=True, vmem_limit_bytes=60 * 1024 * 1024),
    )(queries[0], cache[0, 0], new_kv[0, 0], out_weight, prefix)
    return out[None]


def solution(mesh):
    in_specs = (
        P(("groups", "dp"), None, "tp"),
        P(("groups", "dp"), "tp", None, None, None),
        P(("groups", "dp"), "tp", None, None, None),
        P("tp", None),
        P(("groups", "dp")),
    )
    out_specs = P(("groups", "dp"), None, None)
    return jax.shard_map(
        per_device, mesh=mesh, in_specs=in_specs, out_specs=out_specs, check_vma=False
    )
```

```python
import functools
import math

import jax
import jax.numpy as jnp
from jax import lax
from jax.experimental import pallas as pl
from jax.experimental.pallas import tpu as pltpu
from jax.sharding import PartitionSpec as P

HD = 128
HQ_DEV = 2
CH = 128
SAFE = 896
TILE = 512
WIDE = 256
PARTS = 2
SKEW = 5
BEHIND = 4
MASKED = -1e30
MESH = pl.DeviceIdType.MESH
NT = (((1,), (1,)), ((), ()))


def kernel(n, q_ref, cache_ref, new_ref, w_hbm, prefix_ref, out_ref,
           query2, fresh_kv, kv, weight, scores, attended, parts, stage, landed,
           results, load_sem, rs_send, rs_recv, ag_send, ag_recv):
    t = lax.axis_index("tp")
    pmax = cache_ref.shape[1]
    dw = w_hbm.shape[1]
    half = dw // 2
    per_part = half // WIDE
    count = PARTS * per_part
    deep = CH // PARTS
    has_prev = t > 0
    has_next = t < n - 1
    prev, nxt = jnp.maximum(t - 1, 0), jnp.minimum(t + 1, n - 1)

    loads = [
        pltpu.make_async_copy(q_ref, query2, load_sem.at[6]),
        pltpu.make_async_copy(new_ref, fresh_kv, load_sem.at[7]),
        pltpu.make_async_copy(cache_ref.at[0], kv.at[0], load_sem.at[0]),
        pltpu.make_async_copy(cache_ref.at[1], kv.at[1], load_sem.at[1]),
    ] + [
        pltpu.make_async_copy(w_hbm.at[:, piece], weight.at[:, piece], load_sem.at[2 + j])
        for j, piece in enumerate((
            pl.ds(half, WIDE), pl.ds(0, WIDE),
            pl.ds(half + WIDE, half - WIDE), pl.ds(WIDE, half - WIDE)))
    ]
    barrier = pltpu.get_barrier_semaphore()

    @pl.when(has_prev)
    def _():
        pl.semaphore_signal(barrier, inc=1, device_id={"tp": prev}, device_id_type=MESH)

    @pl.when(has_next)
    def _():
        pl.semaphore_signal(barrier, inc=1, device_id={"tp": nxt}, device_id_type=MESH)

    for load in loads:
        load.start()

    factor = HD ** -0.5 * math.log2(math.e)
    length = prefix_ref[0]
    rows = HQ_DEV * deep

    def widest(top, tile):
        for j in range(tile.shape[1] // 128):
            top = jnp.maximum(top, tile[:, j * 128:(j + 1) * 128])
        return top

    def attend(part):
        mine = slice(part * deep, (part + 1) * deep)
        query = jnp.concatenate([query2[mine, h * HD:(h + 1) * HD] for h in range(HQ_DEV)], axis=0)
        top = jnp.full((rows, 128), MASKED, jnp.float32)
        row = lax.broadcasted_iota(jnp.int32, (rows, CH), 0) % deep + part * deep
        col = lax.broadcasted_iota(jnp.int32, (rows, CH), 1)
        fresh = lax.dot_general(query, fresh_kv[0], NT, preferred_element_type=jnp.float32)
        fresh = jnp.where(col <= row, fresh, MASKED)
        top = widest(top, fresh)
        if part == 0:
            loads[2].wait()
        for start in range(0, pmax, TILE):
            size = min(TILE, pmax - start)
            tile = lax.dot_general(query, kv[0, start:start + size], NT, preferred_element_type=jnp.float32)
            if start + size > SAFE:
                slot = lax.broadcasted_iota(jnp.int32, (1, size), 1) + start
                tile = jnp.where(slot < length, tile, MASKED)
            scores[:, start:start + size] = tile
            top = widest(top, tile)
        highest = jnp.max(top, axis=1, keepdims=True) * factor

        def weigh(tile, total):
            weights = jnp.exp2(tile * factor - highest)
            for j in range(tile.shape[1] // 128):
                total = total + weights[:, j * 128:(j + 1) * 128]
            return weights.astype(jnp.bfloat16), total

        total = jnp.zeros((rows, 128), jnp.float32)
        weights, total = weigh(fresh, total)
        summed = jnp.dot(weights, fresh_kv[1], preferred_element_type=jnp.float32)
        if part == 0:
            loads[3].wait()
        for start in range(0, pmax, TILE):
            size = min(TILE, pmax - start)
            weights, total = weigh(scores[:, start:start + size], total)
            summed = summed + jnp.dot(weights, kv[1, start:start + size], preferred_element_type=jnp.float32)
        summed = summed / jnp.sum(total, axis=1, keepdims=True)
        for h in range(HQ_DEV):
            attended[mine, h * HD:(h + 1) * HD] = summed[h * deep:(h + 1) * deep].astype(jnp.bfloat16)

    loads[0].wait()
    loads[1].wait()

    towards = (nxt, prev)
    back = (prev, nxt)
    is_first = (t == 0, t == n - 1)
    is_owner = (t == n - 1, t == 0)

    def tokens(i):
        return pl.ds(pl.multiple_of(i // per_part * deep, deep), deep)

    def columns(d, i):
        return pl.ds(pl.multiple_of((1 - d) * half + i % per_part * WIDE, WIDE), WIDE)

    def sum_copy(d, i):
        return pltpu.make_async_remote_copy(
            src_ref=stage.at[d, i], dst_ref=landed.at[d, i],
            send_sem=rs_send.at[d, i], recv_sem=rs_recv.at[d, i],
            device_id={"tp": towards[d]}, device_id_type=MESH)

    def result_copy(d, i):
        return pltpu.make_async_remote_copy(
            src_ref=results.at[d, i], dst_ref=results.at[d, i],
            send_sem=ag_send.at[d, i], recv_sem=ag_recv.at[d, i],
            device_id={"tp": back[d]}, device_id_type=MESH)

    early = count - per_part

    def project(d, i):
        @pl.when(jnp.logical_not(is_first[d]) | (i >= early))
        def _():
            parts[d, i] = product(d, i)

    def product(d, i):
        return jnp.dot(attended[tokens(i), :], weight[:, columns(d, i)], preferred_element_type=jnp.float32)

    def sum_step(d, i):
        part = parts[d, i]

        @pl.when(is_first[d] & (i >= early))
        def _():
            stage[d, i] = part.astype(jnp.bfloat16)
            sum_copy(d, i).start()

        @pl.when(jnp.logical_not(is_first[d]))
        def _():
            sum_copy(d, i).wait_recv()
            running = (part + landed[d, i].astype(jnp.float32)).astype(jnp.bfloat16)

            @pl.when(is_owner[d])
            def _():
                results[d, i] = running
                out_ref[tokens(i), columns(d, i)] = running

            @pl.when(jnp.logical_not(is_owner[d]))
            def _():
                stage[d, i] = running
                sum_copy(d, i).start()

    def result_step(d, i):
        @pl.when(is_owner[d])
        def _():
            result_copy(d, i).start()

        @pl.when(jnp.logical_not(is_owner[d]))
        def _():
            result_copy(d, i).wait_recv()

            @pl.when(jnp.logical_not(is_first[d]))
            def _():
                result_copy(d, i).start()

            out_ref[tokens(i), columns(d, i)] = results[d, i]
            sum_copy(d, i).wait_send()

        @pl.when(jnp.logical_not(is_first[d]) & (i >= BEHIND))
        def _():
            result_copy(d, i - BEHIND).wait_send()

    for part in range(PARTS):
        attend(part)
        if part == 0:
            loads[4].wait()
            loads[5].wait()
            for d in range(2):
                @pl.when(is_first[d])
                def _():
                    stage[d, 0] = product(d, 0).astype(jnp.bfloat16)
            pl.semaphore_wait(barrier, has_prev.astype(jnp.int32) + has_next.astype(jnp.int32))
            for d in range(2):
                @pl.when(is_first[d])
                def _():
                    sum_copy(d, 0).start()
            loads[6].wait()
            loads[7].wait()
        if part < PARTS - 1:
            for d in range(2):
                @pl.when(is_first[d])
                def _():
                    @pl.loop(max(part * per_part, 1), (part + 1) * per_part)
                    def _(i):
                        stage[d, i] = product(d, i).astype(jnp.bfloat16)
                        sum_copy(d, i).start()

    far = n - 1
    turn = max(count, far * SKEW)
    hops = (t * SKEW, (far - t) * SKEW)

    @pl.loop(-1, turn + count + far * SKEW)
    def _(step):
        for work, delays in (
            (sum_step, hops),
            (result_step, (turn + hops[1], turn + hops[0])),
            (project, (hops[0] - 1, hops[1] - 1)),
        ):
            for d in range(2):
                i = step - delays[d]

                @pl.when((i >= 0) & (i < count))
                def _():
                    work(d, i)

    @pl.loop(count - min(BEHIND, count), count)
    def _(i):
        for d in range(2):
            @pl.when(jnp.logical_not(is_first[d]))
            def _():
                result_copy(d, i).wait_send()


def per_device(queries, cache, new_kv, out_weight, prefix):
    n = lax.axis_size("tp")
    pmax = cache.shape[3]
    dw = out_weight.shape[1]
    count = PARTS * (dw // 2 // WIDE)
    deep = CH // PARTS
    vmem = pl.BlockSpec(memory_space=pltpu.VMEM)
    hbm = pl.BlockSpec(memory_space=pltpu.HBM)
    out = pl.pallas_call(
        functools.partial(kernel, n),
        out_shape=pltpu.VMEM((CH, dw), jnp.bfloat16),
        in_specs=[hbm, hbm, hbm, hbm, pl.BlockSpec(memory_space=pltpu.SMEM)],
        out_specs=vmem,
        scratch_shapes=[
            pltpu.VMEM((CH, HQ_DEV * HD), jnp.bfloat16),
            pltpu.VMEM((2, CH, HD), jnp.bfloat16),
            pltpu.VMEM((2, pmax, HD), jnp.bfloat16),
            pltpu.VMEM(out_weight.shape, jnp.bfloat16),
            pltpu.VMEM((HQ_DEV * deep, pmax), jnp.float32),
            pltpu.VMEM((CH, HQ_DEV * HD), jnp.bfloat16),
            pltpu.VMEM((2, count, deep, WIDE), jnp.float32),
            pltpu.VMEM((2, count, deep, WIDE), jnp.bfloat16),
            pltpu.VMEM((2, count, deep, WIDE), jnp.bfloat16),
            pltpu.VMEM((2, count, deep, WIDE), jnp.bfloat16),
            pltpu.SemaphoreType.DMA((8,)),
            pltpu.SemaphoreType.DMA((2, count)),
            pltpu.SemaphoreType.DMA((2, count)),
            pltpu.SemaphoreType.DMA((2, count)),
            pltpu.SemaphoreType.DMA((2, count)),
        ],
        compiler_params=pltpu.CompilerParams(
            collective_id=0, has_side_effects=True, vmem_limit_bytes=60 * 1024 * 1024),
    )(queries[0], cache[0, 0], new_kv[0, 0], out_weight, prefix)
    return out[None]


def solution(mesh):
    in_specs = (
        P(("groups", "dp"), None, "tp"),
        P(("groups", "dp"), "tp", None, None, None),
        P(("groups", "dp"), "tp", None, None, None),
        P("tp", None),
        P(("groups", "dp")),
    )
    out_specs = P(("groups", "dp"), None, None)
    return jax.shard_map(
        per_device, mesh=mesh, in_specs=in_specs, out_specs=out_specs, check_vma=False
    )
```

```python
import functools
import math

import jax
import jax.numpy as jnp
from jax import lax
from jax.experimental import pallas as pl
from jax.experimental.pallas import tpu as pltpu
from jax.sharding import PartitionSpec as P

HD = 128
HQ_DEV = 2
CH = 128
SAFE = 896
TILE = 512
WIDE = 512
PARTS = 4
SKEW = 5
BEHIND = 4
MASKED = -1e30
MESH = pl.DeviceIdType.MESH
NT = (((1,), (1,)), ((), ()))


def kernel(n, q_ref, cache_ref, new_ref, w_hbm, prefix_ref, out_ref,
           query2, fresh_kv, kv, weight, scores, attended, parts, stage, landed,
           results, load_sem, rs_send, rs_recv, ag_send, ag_recv):
    t = lax.axis_index("tp")
    pmax = cache_ref.shape[1]
    dw = w_hbm.shape[1]
    half = dw // 2
    per_part = half // WIDE
    count = PARTS * per_part
    deep = CH // PARTS
    has_prev = t > 0
    has_next = t < n - 1
    prev, nxt = jnp.maximum(t - 1, 0), jnp.minimum(t + 1, n - 1)

    loads = [
        pltpu.make_async_copy(q_ref, query2, load_sem.at[6]),
        pltpu.make_async_copy(new_ref, fresh_kv, load_sem.at[7]),
        pltpu.make_async_copy(cache_ref.at[0], kv.at[0], load_sem.at[0]),
        pltpu.make_async_copy(cache_ref.at[1], kv.at[1], load_sem.at[1]),
    ] + [
        pltpu.make_async_copy(w_hbm.at[:, piece], weight.at[:, piece], load_sem.at[2 + j])
        for j, piece in enumerate((
            pl.ds(half, WIDE), pl.ds(0, WIDE),
            pl.ds(half + WIDE, half - WIDE), pl.ds(WIDE, half - WIDE)))
    ]
    barrier = pltpu.get_barrier_semaphore()

    @pl.when(has_prev)
    def _():
        pl.semaphore_signal(barrier, inc=1, device_id={"tp": prev}, device_id_type=MESH)

    @pl.when(has_next)
    def _():
        pl.semaphore_signal(barrier, inc=1, device_id={"tp": nxt}, device_id_type=MESH)

    for load in loads:
        load.start()

    factor = HD ** -0.5 * math.log2(math.e)
    length = prefix_ref[0]
    rows = HQ_DEV * deep

    def widest(top, tile):
        for j in range(tile.shape[1] // 128):
            top = jnp.maximum(top, tile[:, j * 128:(j + 1) * 128])
        return top

    def attend(part):
        mine = slice(part * deep, (part + 1) * deep)
        query = jnp.concatenate([query2[mine, h * HD:(h + 1) * HD] for h in range(HQ_DEV)], axis=0)
        top = jnp.full((rows, 128), MASKED, jnp.float32)
        row = lax.broadcasted_iota(jnp.int32, (rows, CH), 0) % deep + part * deep
        col = lax.broadcasted_iota(jnp.int32, (rows, CH), 1)
        fresh = lax.dot_general(query, fresh_kv[0], NT, preferred_element_type=jnp.float32)
        fresh = jnp.where(col <= row, fresh, MASKED)
        top = widest(top, fresh)
        if part == 0:
            loads[2].wait()
        for start in range(0, pmax, TILE):
            size = min(TILE, pmax - start)
            tile = lax.dot_general(query, kv[0, start:start + size], NT, preferred_element_type=jnp.float32)
            if start + size > SAFE:
                slot = lax.broadcasted_iota(jnp.int32, (1, size), 1) + start
                tile = jnp.where(slot < length, tile, MASKED)
            scores[:, start:start + size] = tile
            top = widest(top, tile)
        highest = jnp.max(top, axis=1, keepdims=True) * factor

        def weigh(tile, total):
            weights = jnp.exp2(tile * factor - highest)
            for j in range(tile.shape[1] // 128):
                total = total + weights[:, j * 128:(j + 1) * 128]
            return weights.astype(jnp.bfloat16), total

        total = jnp.zeros((rows, 128), jnp.float32)
        weights, total = weigh(fresh, total)
        summed = jnp.dot(weights, fresh_kv[1], preferred_element_type=jnp.float32)
        if part == 0:
            loads[3].wait()
        for start in range(0, pmax, TILE):
            size = min(TILE, pmax - start)
            weights, total = weigh(scores[:, start:start + size], total)
            summed = summed + jnp.dot(weights, kv[1, start:start + size], preferred_element_type=jnp.float32)
        summed = summed / jnp.sum(total, axis=1, keepdims=True)
        for h in range(HQ_DEV):
            attended[mine, h * HD:(h + 1) * HD] = summed[h * deep:(h + 1) * deep].astype(jnp.bfloat16)

    loads[0].wait()
    loads[1].wait()

    towards = (nxt, prev)
    back = (prev, nxt)
    is_first = (t == 0, t == n - 1)
    is_owner = (t == n - 1, t == 0)

    def tokens(i):
        return pl.ds(pl.multiple_of(i // per_part * deep, deep), deep)

    def columns(d, i):
        return pl.ds(pl.multiple_of((1 - d) * half + i % per_part * WIDE, WIDE), WIDE)

    def sum_copy(d, i):
        return pltpu.make_async_remote_copy(
            src_ref=stage.at[d, i], dst_ref=landed.at[d, i],
            send_sem=rs_send.at[d, i], recv_sem=rs_recv.at[d, i],
            device_id={"tp": towards[d]}, device_id_type=MESH)

    def result_copy(d, i):
        return pltpu.make_async_remote_copy(
            src_ref=results.at[d, i], dst_ref=results.at[d, i],
            send_sem=ag_send.at[d, i], recv_sem=ag_recv.at[d, i],
            device_id={"tp": back[d]}, device_id_type=MESH)

    early = count - per_part

    def project(d, i):
        @pl.when(jnp.logical_not(is_first[d]) | (i >= early))
        def _():
            parts[d, i] = product(d, i)

    def product(d, i):
        return jnp.dot(attended[tokens(i), :], weight[:, columns(d, i)], preferred_element_type=jnp.float32)

    def sum_step(d, i):
        part = parts[d, i]

        @pl.when(is_first[d] & (i >= early))
        def _():
            stage[d, i] = part.astype(jnp.bfloat16)
            sum_copy(d, i).start()

        @pl.when(jnp.logical_not(is_first[d]))
        def _():
            sum_copy(d, i).wait_recv()
            running = (part + landed[d, i].astype(jnp.float32)).astype(jnp.bfloat16)

            @pl.when(is_owner[d])
            def _():
                results[d, i] = running
                out_ref[tokens(i), columns(d, i)] = running

            @pl.when(jnp.logical_not(is_owner[d]))
            def _():
                stage[d, i] = running
                sum_copy(d, i).start()

    def result_step(d, i):
        @pl.when(is_owner[d])
        def _():
            result_copy(d, i).start()

        @pl.when(jnp.logical_not(is_owner[d]))
        def _():
            result_copy(d, i).wait_recv()

            @pl.when(jnp.logical_not(is_first[d]))
            def _():
                result_copy(d, i).start()

            out_ref[tokens(i), columns(d, i)] = results[d, i]
            sum_copy(d, i).wait_send()

        @pl.when(jnp.logical_not(is_first[d]) & (i >= BEHIND))
        def _():
            result_copy(d, i - BEHIND).wait_send()

    for part in range(PARTS):
        attend(part)
        if part == 0:
            loads[4].wait()
            loads[5].wait()
            for d in range(2):
                @pl.when(is_first[d])
                def _():
                    stage[d, 0] = product(d, 0).astype(jnp.bfloat16)
            pl.semaphore_wait(barrier, has_prev.astype(jnp.int32) + has_next.astype(jnp.int32))
            for d in range(2):
                @pl.when(is_first[d])
                def _():
                    sum_copy(d, 0).start()
            loads[6].wait()
            loads[7].wait()
        if part < PARTS - 1:
            for d in range(2):
                @pl.when(is_first[d])
                def _():
                    @pl.loop(max(part * per_part, 1), (part + 1) * per_part)
                    def _(i):
                        stage[d, i] = product(d, i).astype(jnp.bfloat16)
                        sum_copy(d, i).start()

    far = n - 1
    turn = max(count, far * SKEW)
    hops = (t * SKEW, (far - t) * SKEW)

    @pl.loop(-1, turn + count + far * SKEW)
    def _(step):
        for work, delays in (
            (sum_step, hops),
            (result_step, (turn + hops[1], turn + hops[0])),
            (project, (hops[0] - 1, hops[1] - 1)),
        ):
            for d in range(2):
                i = step - delays[d]

                @pl.when((i >= 0) & (i < count))
                def _():
                    work(d, i)

    @pl.loop(count - min(BEHIND, count), count)
    def _(i):
        for d in range(2):
            @pl.when(jnp.logical_not(is_first[d]))
            def _():
                result_copy(d, i).wait_send()


def per_device(queries, cache, new_kv, out_weight, prefix):
    n = lax.axis_size("tp")
    pmax = cache.shape[3]
    dw = out_weight.shape[1]
    count = PARTS * (dw // 2 // WIDE)
    deep = CH // PARTS
    vmem = pl.BlockSpec(memory_space=pltpu.VMEM)
    hbm = pl.BlockSpec(memory_space=pltpu.HBM)
    out = pl.pallas_call(
        functools.partial(kernel, n),
        out_shape=pltpu.VMEM((CH, dw), jnp.bfloat16),
        in_specs=[hbm, hbm, hbm, hbm, pl.BlockSpec(memory_space=pltpu.SMEM)],
        out_specs=vmem,
        scratch_shapes=[
            pltpu.VMEM((CH, HQ_DEV * HD), jnp.bfloat16),
            pltpu.VMEM((2, CH, HD), jnp.bfloat16),
            pltpu.VMEM((2, pmax, HD), jnp.bfloat16),
            pltpu.VMEM(out_weight.shape, jnp.bfloat16),
            pltpu.VMEM((HQ_DEV * deep, pmax), jnp.float32),
            pltpu.VMEM((CH, HQ_DEV * HD), jnp.bfloat16),
            pltpu.VMEM((2, count, deep, WIDE), jnp.float32),
            pltpu.VMEM((2, count, deep, WIDE), jnp.bfloat16),
            pltpu.VMEM((2, count, deep, WIDE), jnp.bfloat16),
            pltpu.VMEM((2, count, deep, WIDE), jnp.bfloat16),
            pltpu.SemaphoreType.DMA((8,)),
            pltpu.SemaphoreType.DMA((2, count)),
            pltpu.SemaphoreType.DMA((2, count)),
            pltpu.SemaphoreType.DMA((2, count)),
            pltpu.SemaphoreType.DMA((2, count)),
        ],
        compiler_params=pltpu.CompilerParams(
            collective_id=0, has_side_effects=True, vmem_limit_bytes=60 * 1024 * 1024),
    )(queries[0], cache[0, 0], new_kv[0, 0], out_weight, prefix)
    return out[None]


def solution(mesh):
    in_specs = (
        P(("groups", "dp"), None, "tp"),
        P(("groups", "dp"), "tp", None, None, None),
        P(("groups", "dp"), "tp", None, None, None),
        P("tp", None),
        P(("groups", "dp")),
    )
    out_specs = P(("groups", "dp"), None, None)
    return jax.shard_map(
        per_device, mesh=mesh, in_specs=in_specs, out_specs=out_specs, check_vma=False
    )
```

```python
import functools
import math

import jax
import jax.numpy as jnp
from jax import lax
from jax.experimental import pallas as pl
from jax.experimental.pallas import tpu as pltpu
from jax.sharding import PartitionSpec as P

HD = 128
HQ_DEV = 2
CH = 128
SAFE = 896
TILE = 896
WIDE = 512
PARTS = 4
SKEW = 5
BEHIND = 4
MASKED = -1e30
MESH = pl.DeviceIdType.MESH
NT = (((1,), (1,)), ((), ()))


def kernel(n, q_ref, cache_ref, new_ref, w_hbm, prefix_ref, out_ref,
           query2, fresh_kv, kv, weight, scores, attended, parts, stage, landed,
           results, load_sem, rs_send, rs_recv, ag_send, ag_recv):
    t = lax.axis_index("tp")
    pmax = cache_ref.shape[1]
    dw = w_hbm.shape[1]
    half = dw // 2
    per_part = half // WIDE
    count = PARTS * per_part
    deep = CH // PARTS
    has_prev = t > 0
    has_next = t < n - 1
    prev, nxt = jnp.maximum(t - 1, 0), jnp.minimum(t + 1, n - 1)

    loads = [
        pltpu.make_async_copy(q_ref, query2, load_sem.at[6]),
        pltpu.make_async_copy(new_ref, fresh_kv, load_sem.at[7]),
        pltpu.make_async_copy(cache_ref.at[0], kv.at[0], load_sem.at[0]),
        pltpu.make_async_copy(cache_ref.at[1], kv.at[1], load_sem.at[1]),
    ] + [
        pltpu.make_async_copy(w_hbm.at[:, piece], weight.at[:, piece], load_sem.at[2 + j])
        for j, piece in enumerate((
            pl.ds(half, WIDE), pl.ds(0, WIDE),
            pl.ds(half + WIDE, half - WIDE), pl.ds(WIDE, half - WIDE)))
    ]
    barrier = pltpu.get_barrier_semaphore()

    @pl.when(has_prev)
    def _():
        pl.semaphore_signal(barrier, inc=1, device_id={"tp": prev}, device_id_type=MESH)

    @pl.when(has_next)
    def _():
        pl.semaphore_signal(barrier, inc=1, device_id={"tp": nxt}, device_id_type=MESH)

    for load in loads:
        load.start()

    factor = HD ** -0.5 * math.log2(math.e)
    length = prefix_ref[0]
    rows = HQ_DEV * deep

    def widest(top, tile):
        for j in range(tile.shape[1] // 128):
            top = jnp.maximum(top, tile[:, j * 128:(j + 1) * 128])
        return top

    def attend(part):
        mine = slice(part * deep, (part + 1) * deep)
        query = jnp.concatenate([query2[mine, h * HD:(h + 1) * HD] for h in range(HQ_DEV)], axis=0)
        top = jnp.full((rows, 128), MASKED, jnp.float32)
        row = lax.broadcasted_iota(jnp.int32, (rows, CH), 0) % deep + part * deep
        col = lax.broadcasted_iota(jnp.int32, (rows, CH), 1)
        fresh = lax.dot_general(query, fresh_kv[0], NT, preferred_element_type=jnp.float32)
        fresh = jnp.where(col <= row, fresh, MASKED)
        top = widest(top, fresh)
        if part == 0:
            loads[2].wait()
        for start in range(0, pmax, TILE):
            size = min(TILE, pmax - start)
            tile = lax.dot_general(query, kv[0, start:start + size], NT, preferred_element_type=jnp.float32)
            if start + size > SAFE:
                slot = lax.broadcasted_iota(jnp.int32, (1, size), 1) + start
                tile = jnp.where(slot < length, tile, MASKED)
            scores[:, start:start + size] = tile
            top = widest(top, tile)
        highest = jnp.max(top, axis=1, keepdims=True) * factor

        def weigh(tile, total):
            weights = jnp.exp2(tile * factor - highest)
            for j in range(tile.shape[1] // 128):
                total = total + weights[:, j * 128:(j + 1) * 128]
            return weights.astype(jnp.bfloat16), total

        total = jnp.zeros((rows, 128), jnp.float32)
        weights, total = weigh(fresh, total)
        summed = jnp.dot(weights, fresh_kv[1], preferred_element_type=jnp.float32)
        if part == 0:
            loads[3].wait()
        for start in range(0, pmax, TILE):
            size = min(TILE, pmax - start)
            weights, total = weigh(scores[:, start:start + size], total)
            summed = summed + jnp.dot(weights, kv[1, start:start + size], preferred_element_type=jnp.float32)
        summed = summed / jnp.sum(total, axis=1, keepdims=True)
        for h in range(HQ_DEV):
            attended[mine, h * HD:(h + 1) * HD] = summed[h * deep:(h + 1) * deep].astype(jnp.bfloat16)

    loads[0].wait()
    loads[1].wait()

    towards = (nxt, prev)
    back = (prev, nxt)
    is_first = (t == 0, t == n - 1)
    is_owner = (t == n - 1, t == 0)

    def tokens(i):
        return pl.ds(pl.multiple_of(i // per_part * deep, deep), deep)

    def columns(d, i):
        return pl.ds(pl.multiple_of((1 - d) * half + i % per_part * WIDE, WIDE), WIDE)

    def sum_copy(d, i):
        return pltpu.make_async_remote_copy(
            src_ref=stage.at[d, i], dst_ref=landed.at[d, i],
            send_sem=rs_send.at[d, i], recv_sem=rs_recv.at[d, i],
            device_id={"tp": towards[d]}, device_id_type=MESH)

    def result_copy(d, i):
        return pltpu.make_async_remote_copy(
            src_ref=results.at[d, i], dst_ref=results.at[d, i],
            send_sem=ag_send.at[d, i], recv_sem=ag_recv.at[d, i],
            device_id={"tp": back[d]}, device_id_type=MESH)

    early = count - per_part

    def project(d, i):
        @pl.when(jnp.logical_not(is_first[d]) | (i >= early))
        def _():
            parts[d, i] = product(d, i)

    def product(d, i):
        return jnp.dot(attended[tokens(i), :], weight[:, columns(d, i)], preferred_element_type=jnp.float32)

    def sum_step(d, i):
        part = parts[d, i]

        @pl.when(is_first[d] & (i >= early))
        def _():
            stage[d, i] = part.astype(jnp.bfloat16)
            sum_copy(d, i).start()

        @pl.when(jnp.logical_not(is_first[d]))
        def _():
            sum_copy(d, i).wait_recv()
            running = (part + landed[d, i].astype(jnp.float32)).astype(jnp.bfloat16)

            @pl.when(is_owner[d])
            def _():
                results[d, i] = running
                out_ref[tokens(i), columns(d, i)] = running

            @pl.when(jnp.logical_not(is_owner[d]))
            def _():
                stage[d, i] = running
                sum_copy(d, i).start()

    def result_step(d, i):
        @pl.when(is_owner[d])
        def _():
            result_copy(d, i).start()

        @pl.when(jnp.logical_not(is_owner[d]))
        def _():
            result_copy(d, i).wait_recv()

            @pl.when(jnp.logical_not(is_first[d]))
            def _():
                result_copy(d, i).start()

            out_ref[tokens(i), columns(d, i)] = results[d, i]
            sum_copy(d, i).wait_send()

        @pl.when(jnp.logical_not(is_first[d]) & (i >= BEHIND))
        def _():
            result_copy(d, i - BEHIND).wait_send()

    for part in range(PARTS):
        attend(part)
        if part == 0:
            loads[4].wait()
            loads[5].wait()
            for d in range(2):
                @pl.when(is_first[d])
                def _():
                    stage[d, 0] = product(d, 0).astype(jnp.bfloat16)
            pl.semaphore_wait(barrier, has_prev.astype(jnp.int32) + has_next.astype(jnp.int32))
            for d in range(2):
                @pl.when(is_first[d])
                def _():
                    sum_copy(d, 0).start()
            loads[6].wait()
            loads[7].wait()
        if part < PARTS - 1:
            for d in range(2):
                @pl.when(is_first[d])
                def _():
                    @pl.loop(max(part * per_part, 1), (part + 1) * per_part)
                    def _(i):
                        stage[d, i] = product(d, i).astype(jnp.bfloat16)
                        sum_copy(d, i).start()

    far = n - 1
    turn = max(count, far * SKEW)
    hops = (t * SKEW, (far - t) * SKEW)

    @pl.loop(-1, turn + count + far * SKEW)
    def _(step):
        for work, delays in (
            (sum_step, hops),
            (result_step, (turn + hops[1], turn + hops[0])),
            (project, (hops[0] - 1, hops[1] - 1)),
        ):
            for d in range(2):
                i = step - delays[d]

                @pl.when((i >= 0) & (i < count))
                def _():
                    work(d, i)

    @pl.loop(count - min(BEHIND, count), count)
    def _(i):
        for d in range(2):
            @pl.when(jnp.logical_not(is_first[d]))
            def _():
                result_copy(d, i).wait_send()


def per_device(queries, cache, new_kv, out_weight, prefix):
    n = lax.axis_size("tp")
    pmax = cache.shape[3]
    dw = out_weight.shape[1]
    count = PARTS * (dw // 2 // WIDE)
    deep = CH // PARTS
    vmem = pl.BlockSpec(memory_space=pltpu.VMEM)
    hbm = pl.BlockSpec(memory_space=pltpu.HBM)
    out = pl.pallas_call(
        functools.partial(kernel, n),
        out_shape=pltpu.VMEM((CH, dw), jnp.bfloat16),
        in_specs=[hbm, hbm, hbm, hbm, pl.BlockSpec(memory_space=pltpu.SMEM)],
        out_specs=vmem,
        scratch_shapes=[
            pltpu.VMEM((CH, HQ_DEV * HD), jnp.bfloat16),
            pltpu.VMEM((2, CH, HD), jnp.bfloat16),
            pltpu.VMEM((2, pmax, HD), jnp.bfloat16),
            pltpu.VMEM(out_weight.shape, jnp.bfloat16),
            pltpu.VMEM((HQ_DEV * deep, pmax), jnp.float32),
            pltpu.VMEM((CH, HQ_DEV * HD), jnp.bfloat16),
            pltpu.VMEM((2, count, deep, WIDE), jnp.float32),
            pltpu.VMEM((2, count, deep, WIDE), jnp.bfloat16),
            pltpu.VMEM((2, count, deep, WIDE), jnp.bfloat16),
            pltpu.VMEM((2, count, deep, WIDE), jnp.bfloat16),
            pltpu.SemaphoreType.DMA((8,)),
            pltpu.SemaphoreType.DMA((2, count)),
            pltpu.SemaphoreType.DMA((2, count)),
            pltpu.SemaphoreType.DMA((2, count)),
            pltpu.SemaphoreType.DMA((2, count)),
        ],
        compiler_params=pltpu.CompilerParams(
            collective_id=0, has_side_effects=True, vmem_limit_bytes=60 * 1024 * 1024),
    )(queries[0], cache[0, 0], new_kv[0, 0], out_weight, prefix)
    return out[None]


def solution(mesh):
    in_specs = (
        P(("groups", "dp"), None, "tp"),
        P(("groups", "dp"), "tp", None, None, None),
        P(("groups", "dp"), "tp", None, None, None),
        P("tp", None),
        P(("groups", "dp")),
    )
    out_specs = P(("groups", "dp"), None, None)
    return jax.shard_map(
        per_device, mesh=mesh, in_specs=in_specs, out_specs=out_specs, check_vma=False
    )
```
